32 devices in a mesh: ctx: 8 (over y, x, core), grp: 4 (over z).
Axes of the slice: x: 2, y: 2, z: 4, core: 2. Of those that a mesh axis runs over, the one named last changes fastest.
Arguments:
- queries: bfloat16 [8192, 128], P(('grp', 'ctx')), parts along dimension 0, may hold values from -6 to 6
- keys: bfloat16 [8192, 128], P(('grp', 'ctx')), parts along dimension 0, may hold values from -6 to 6
- values: bfloat16 [8192, 128], P(('grp', 'ctx')), parts along dimension 0, may hold values from -6 to 6
- grad_out: bfloat16 [8192, 128], P(('grp', 'ctx')), parts along dimension 0, may hold values from -6 to 6
Outputs:
- output: bfloat16 [8192, 128], P(('grp', 'ctx')), parts along dimension 0
- grad_query: bfloat16 [8192, 128], P(('grp', 'ctx')), parts along dimension 0
- grad_key: bfloat16 [8192, 128], P(('grp', 'ctx')), parts along dimension 0
- grad_value: bfloat16 [8192, 128], P(('grp', 'ctx')), parts along dimension 0
The draws below stay inside these ranges and needn't reach their ends.
There are 4 independent parts, one for each index of `grp`. The reference program is written for one: setup_inputs(seed, part) draws one part's arguments, and reference() takes and returns one part's arrays. A program takes and returns all parts, laid end to end along the dimension named above; each array names one. Nothing has to cross between parts.
All inputs are finite; a program needn't handle non-finite values.
Results may differ from the reference program's by a relative error of at most 0.025.
Values may be sent and summed in bfloat16 or wider, within the bound.
A program may use at most 64 MiB of HBM per device.

```python
import math
import jax
import jax.numpy as jnp
from jax import lax

D_HEAD = 128
TOK_DEV = 256
TOKENS = 2048


def shared_lean(key):
    signs = jax.random.normal(jax.random.fold_in(key, 17), (D_HEAD,), jnp.float32)
    amount = math.sqrt(4.0 / math.sqrt(D_HEAD))
    return jnp.where(signs > 0, amount, -amount)


def draw_queries(key, part):
    lean = shared_lean(key)
    key = jax.random.fold_in(key, 5)
    drawn = jax.random.normal(key, (TOKENS, D_HEAD), jnp.float32) + lean[None, :]
    return jnp.clip(drawn, -6.0, 6.0).astype(jnp.bfloat16)


def draw_keys(key, part):
    lean = shared_lean(key)
    key = jax.random.fold_in(key, 3)
    rows = jnp.arange(TOKENS)
    first = (rows < TOK_DEV).astype(jnp.float32)
    drawn = jax.random.normal(key, (TOKENS, D_HEAD), jnp.float32) + first[:, None] * lean[None, :]
    return jnp.clip(drawn, -6.0, 6.0).astype(jnp.bfloat16)


def level_of(stream_key, shape, split, low, top_value):
    def one(axis_at, blocks):
        heights = jax.random.uniform(jax.random.fold_in(jax.random.fold_in(stream_key, 6), axis_at), (blocks,), jnp.float32, low / len(split), top_value / len(split))
        return jnp.repeat(jnp.exp(heights), shape[axis_at] // blocks).reshape((-1,) + (1,) * (len(shape) - axis_at - 1))

    factor_of = one(*split[0])
    for cut in split[1:]:
        factor_of = factor_of * one(*cut)
    return factor_of


def centred(stream_key, shape, scale, most, cuts=(), kind=jnp.bfloat16):
    entries = jax.random.normal(stream_key, shape, jnp.float32) * scale
    if len(cuts) > 0:
        entries = level_of(stream_key, shape, cuts, -0.22, 0.18) * entries
    return jnp.clip(entries, min=-most, max=most).astype(kind)


def setup_inputs(seed: int = 0, part: int = 0) -> dict:
    streams_of = jax.random.split(jax.random.key(seed), 5)
    own_keys = jax.random.split(jax.random.fold_in(streams_of[4], part), 5)
    queries = draw_queries(jax.random.fold_in(jax.random.fold_in(streams_of[4], part), 71), part)
    keys = draw_keys(jax.random.fold_in(jax.random.fold_in(streams_of[4], part), 71), part)
    values = centred(own_keys[2], (TOKENS, D_HEAD), 1.0, 6.0, ((0, 8),))
    grad_out = centred(own_keys[3], (TOKENS, D_HEAD), 1.0, 6.0, ((0, 8),))
    return {"queries": queries, "keys": keys, "values": values, "grad_out": grad_out}


def reference(queries, keys, values, grad_out):
    factor = 1.0 / math.sqrt(D_HEAD)
    width = min(512, TOKENS)
    count = TOKENS // width
    positions = jnp.arange(TOKENS, dtype=jnp.int32)

    def scores_for(first):
        query_block = lax.dynamic_slice_in_dim(queries, first, width, 0)
        own_pos = lax.dynamic_slice_in_dim(positions, first, width, 0)
        scores = jnp.dot(query_block, keys.T, preferred_element_type=jnp.float32) * factor
        allowed = positions[None, :] <= own_pos[:, None]
        return (query_block, scores, allowed)

    def forward_block(index):
        first = (index * width).astype(jnp.int32)
        _, scores, allowed = scores_for(first)
        peak = lax.optimization_barrier(jnp.max(jnp.where(allowed, scores, -jnp.inf), axis=1))
        total = lax.optimization_barrier(jnp.sum(jnp.exp(jnp.where(allowed, scores - peak[:, None], -jnp.inf)), axis=1))
        log_total = peak + jnp.log(total)
        weights = jnp.exp(jnp.where(allowed, scores - log_total[:, None], -jnp.inf)).astype(jnp.bfloat16)
        output = jnp.dot(weights, values, preferred_element_type=jnp.float32).astype(jnp.bfloat16)
        return (output, log_total)
    output, log_total = lax.map(forward_block, jnp.arange(count, dtype=jnp.int32))
    output = output.reshape(TOKENS, D_HEAD)
    log_total = log_total.reshape(TOKENS)
    row_delta = lax.optimization_barrier(jnp.sum(grad_out.astype(jnp.float32) * output.astype(jnp.float32), axis=1))

    def backward_block(carry, index):
        grad_keys, grad_values = carry
        first = (index * width).astype(jnp.int32)
        query_block, scores, allowed = scores_for(first)
        grad_block = lax.dynamic_slice_in_dim(grad_out, first, width, 0)
        block_total = lax.dynamic_slice_in_dim(log_total, first, width, 0)
        block_delta = lax.dynamic_slice_in_dim(row_delta, first, width, 0)
        probs = jnp.exp(jnp.where(allowed, scores - block_total[:, None], -jnp.inf))
        grad_probs = jnp.dot(grad_block, values.T, preferred_element_type=jnp.float32)
        grad_scores = (probs * (grad_probs - block_delta[:, None])).astype(jnp.bfloat16)
        grad_values = grad_values + jnp.dot(probs.astype(jnp.bfloat16).T, grad_block, preferred_element_type=jnp.float32)
        grad_keys = grad_keys + jnp.dot(grad_scores.T, query_block, preferred_element_type=jnp.float32)
        grad_query = (jnp.dot(grad_scores, keys, preferred_element_type=jnp.float32) * factor).astype(jnp.bfloat16)
        return ((grad_keys, grad_values), grad_query)
    empty = jnp.zeros((TOKENS, D_HEAD), jnp.float32)
    sums, grad_query = lax.scan(backward_block, (empty, empty), jnp.arange(count, dtype=jnp.int32))
    grad_key = (sums[0] * factor).astype(jnp.bfloat16)
    grad_value = sums[1].astype(jnp.bfloat16)
    return (output, grad_query.reshape(TOKENS, D_HEAD), grad_key, grad_value)
```

```python
import functools
import math

import jax
import jax.numpy as jnp
from jax import lax
from jax.experimental import pallas as pl
from jax.experimental.pallas import tpu as pltpu
from jax.sharding import PartitionSpec as P

MESH = pl.DeviceIdType.MESH
LOWEST = -1e30
NT = (((1,), (1,)), ((), ()))


def flip(index, by, count):
    result = 0
    bit = 1
    while bit < count:
        both = (index // bit) % 2 + (by // bit) % 2
        result = result + (both % 2) * bit
        bit *= 2
    return result


def kernel(
    n, q_hbm, k_hbm, v_hbm, g_hbm, o_hbm, dq_hbm, dk_hbm, dv_hbm,
    own, slots, raw, graw, stats, peak, total, accum, dq, dk, dv, outs,
    load_sem, send_sem, recv_sem, relay_sem, stat_send, stat_recv, store_sem,
):
    rows, width = q_hbm.shape
    factor = 1.0 / math.sqrt(width)
    scale = factor * math.log2(math.e)
    me = lax.axis_index("ctx")
    chips = n // 2
    chip, core = me // 2, me % 2
    sibling = chip * 2 + 1 - core
    Q, K, V, G = 0, 1, 2, 3

    loads = [
        pltpu.make_async_copy(src, own.at[i], load_sem.at[i])
        for i, src in enumerate((q_hbm, k_hbm, v_hbm, g_hbm))
    ]
    for load in loads:
        load.start()
    barrier = pltpu.get_barrier_semaphore()

    def greet(step, carry):
        other = (me + step) % n
        pl.semaphore_signal(barrier, inc=1, device_id={"ctx": other}, device_id_type=MESH)
        return carry

    lax.fori_loop(1, n, greet, 0)
    for load in loads:
        load.wait()
    pl.semaphore_wait(barrier, n - 1)

    def send_copy(part, other):
        above = (other > me).astype(jnp.int32)
        first = above * (K if part == 0 else V) + (1 - above) * (Q if part == 0 else G)
        return pltpu.make_async_remote_copy(
            src_ref=own.at[first],
            dst_ref=slots.at[me, part],
            send_sem=send_sem.at[other, part],
            recv_sem=recv_sem.at[me, part],
            device_id={"ctx": other},
            device_id_type=MESH,
        )

    def arrival(source, part):
        return pltpu.make_async_remote_copy(
            src_ref=slots.at[source, part],
            dst_ref=slots.at[source, part],
            send_sem=relay_sem.at[source, part],
            recv_sem=recv_sem.at[source, part],
            device_id={"ctx": sibling},
            device_id_type=MESH,
        )

    def send_all(step, carry):
        other = flip(chip, step, chips) * 2 + core
        send_copy(0, other).start()
        send_copy(1, other).start()
        return carry

    lax.fori_loop(1, chips, send_all, 0)
    send_copy(0, sibling).start()
    send_copy(1, sibling).start()

    def dot(a, b):
        return jnp.dot(a, b, preferred_element_type=jnp.float32)

    def dot_nt(a, b):
        return lax.dot_general(a, b, NT, preferred_element_type=jnp.float32)

    row = lax.broadcasted_iota(jnp.int32, (rows, rows), 0)
    col = lax.broadcasted_iota(jnp.int32, (rows, rows), 1)
    scores = jnp.where(col <= row, dot_nt(own[Q], own[K]) * scale, LOWEST)
    raw[me] = scores
    graw[me] = dot_nt(own[G], own[V])
    top = jnp.max(scores, axis=1, keepdims=True)
    probs = jnp.exp2(scores - top)
    peak[...] = jnp.broadcast_to(top, peak.shape)
    total[...] = jnp.broadcast_to(jnp.sum(probs, axis=1, keepdims=True), total.shape)
    accum[...] = dot(probs.astype(jnp.bfloat16), own[V])
    raw[n] = jnp.where(row <= col, dot_nt(own[K], own[Q]) * scale, LOWEST)
    graw[n] = dot_nt(own[V], own[G])

    def take(source):
        above = (source > me).astype(jnp.int32)
        left = own[above * K + (1 - above) * Q]
        right = own[above * V + (1 - above) * G]
        scores = dot_nt(left, slots[source, 0]) * scale
        raw[source] = scores
        graw[source] = dot_nt(right, slots[source, 1])

        @pl.when(source < me)
        def _():
            before = peak[...]
            s = raw[source]
            top = jnp.maximum(before, jnp.max(s, axis=1, keepdims=True))
            decay = jnp.exp2(before - top)
            probs = jnp.exp2(s - top[:, :1])
            peak[...] = top
            total[...] = total[...] * decay + jnp.sum(probs, axis=1, keepdims=True)
            accum[...] = accum[...] * decay[:, :1] + dot(
                probs.astype(jnp.bfloat16), slots[source, 1]
            )

    for part in range(2):
        arrival(sibling, part).wait_recv()
    take(sibling)

    def receive(step, carry):
        far = flip(chip, step, chips) * 2
        for part in range(2):
            arrival(far + core, part).wait_recv()
            arrival(far + core, part).start()
        take(far + core)
        for part in range(2):
            arrival(far + 1 - core, part).wait_recv()
        take(far + 1 - core)
        return carry

    lax.fori_loop(1, chips, receive, 0)

    log_total = peak[:, :1] + jnp.log2(total[:, :1])
    out = (accum[...] / total[:, :1]).astype(jnp.bfloat16)
    outs[0] = out
    delta = jnp.sum(own[G].astype(jnp.float32) * out.astype(jnp.float32), axis=1, keepdims=True)
    lane = lax.broadcasted_iota(jnp.int32, (rows, 128), 1)
    both = jnp.where(lane < 8, log_total, delta)
    stats[me] = jnp.transpose(both)[:16, :]
    store_out = pltpu.make_async_copy(outs.at[0], o_hbm, store_sem.at[0])
    store_out.start()

    def stat_copy(source, other):
        return pltpu.make_async_remote_copy(
            src_ref=stats.at[source],
            dst_ref=stats.at[source],
            send_sem=stat_send.at[other],
            recv_sem=stat_recv.at[source],
            device_id={"ctx": other},
            device_id_type=MESH,
        )

    def send_stats(other, carry):
        stat_copy(me, other).start()
        return carry

    lax.fori_loop(0, me, send_stats, 0)

    peak[...] = jnp.broadcast_to(log_total, peak.shape)
    total[...] = jnp.broadcast_to(delta, total.shape)

    def query_block(source, keys):
        probs = jnp.exp2(raw[source] - peak[:, :1])
        return dot((probs * (graw[source] - total[:, :1])).astype(jnp.bfloat16), keys)

    dq[...] = query_block(me, own[K])

    def query_step(source, carry):
        dq[...] += query_block(source, slots[source, 0])
        return carry

    lax.fori_loop(0, me, query_step, 0)
    outs[1] = (dq[...] * factor).astype(jnp.bfloat16)
    store_dq = pltpu.make_async_copy(outs.at[1], dq_hbm, store_sem.at[1])
    store_dq.start()

    def key_block(place, source, queries, grads):
        probs = jnp.exp2(raw[place] - stats[source, 0:1, :])
        gvalue = dot(probs.astype(jnp.bfloat16), grads)
        ds = (probs * (graw[place] - stats[source, 8:9, :])).astype(jnp.bfloat16)
        return dot(ds, queries), gvalue

    gk, gv = key_block(n, me, own[Q], own[G])
    dk[...] = gk
    dv[...] = gv

    def key_step(source, carry):
        stat_copy(source, sibling).wait_recv()
        gk, gv = key_block(source, source, slots[source, 0], slots[source, 1])
        dk[...] += gk
        dv[...] += gv
        return carry

    lax.fori_loop(me + 1, n, key_step, 0)
    outs[2] = (dk[...] * factor).astype(jnp.bfloat16)
    outs[3] = dv[...].astype(jnp.bfloat16)
    store_dk = pltpu.make_async_copy(outs.at[2], dk_hbm, store_sem.at[2])
    store_dv = pltpu.make_async_copy(outs.at[3], dv_hbm, store_sem.at[3])
    store_dk.start()
    store_dv.start()

    def drain(step, carry):
        far = flip(chip, step, chips) * 2 + core
        for part in range(2):
            send_copy(part, far).wait_send()
            arrival(far, part).wait_send()
        return carry

    lax.fori_loop(1, chips, drain, 0)
    for part in range(2):
        send_copy(part, sibling).wait_send()

    def drain_stats(other, carry):
        stat_copy(me, other).wait_send()
        return carry

    lax.fori_loop(0, me, drain_stats, 0)
    store_out.wait()
    store_dq.wait()
    store_dk.wait()
    store_dv.wait()


def shards(n, queries, keys, values, grad_out):
    rows, width = queries.shape
    shape = jax.ShapeDtypeStruct((rows, width), jnp.bfloat16)
    f32 = jnp.float32
    return pl.pallas_call(
        functools.partial(kernel, n),
        out_shape=(shape,) * 4,
        in_specs=[pl.BlockSpec(memory_space=pltpu.HBM)] * 4,
        out_specs=(pl.BlockSpec(memory_space=pltpu.HBM),) * 4,
        scratch_shapes=[
            pltpu.VMEM((4, rows, width), jnp.bfloat16),
            pltpu.VMEM((n, 2, rows, width), jnp.bfloat16),
            pltpu.VMEM((n + 1, rows, rows), f32),
            pltpu.VMEM((n + 1, rows, rows), f32),
            pltpu.VMEM((n, 16, rows), f32),
            pltpu.VMEM((rows, 128), f32),
            pltpu.VMEM((rows, 128), f32),
            pltpu.VMEM((rows, width), f32),
            pltpu.VMEM((rows, width), f32),
            pltpu.VMEM((rows, width), f32),
            pltpu.VMEM((rows, width), f32),
            pltpu.VMEM((4, rows, width), jnp.bfloat16),
            pltpu.SemaphoreType.DMA((4,)),
            pltpu.SemaphoreType.DMA((n, 2)),
            pltpu.SemaphoreType.DMA((n, 2)),
            pltpu.SemaphoreType.DMA((n, 2)),
            pltpu.SemaphoreType.DMA((n,)),
            pltpu.SemaphoreType.DMA((n,)),
            pltpu.SemaphoreType.DMA((4,)),
        ],
        compiler_params=pltpu.CompilerParams(
            collective_id=0,
            has_side_effects=True,
            vmem_limit_bytes=60 * 1024 * 1024,
        ),
    )(queries, keys, values, grad_out)


def solution(mesh):
    placed = P(("grp", "ctx"), None)
    return jax.shard_map(
        functools.partial(shards, mesh.shape["ctx"]),
        mesh=mesh,
        in_specs=(placed,) * 4,
        out_specs=(placed,) * 4,
        check_vma=False,
    )
```

```python
import functools
import math

import jax
import jax.numpy as jnp
from jax import lax
from jax.experimental import pallas as pl
from jax.experimental.pallas import tpu as pltpu
from jax.sharding import PartitionSpec as P

MESH = pl.DeviceIdType.MESH
LOWEST = -1e30
NT = (((1,), (1,)), ((), ()))


def flip(index, by, count):
    result = 0
    bit = 1
    while bit < count:
        both = (index // bit) % 2 + (by // bit) % 2
        result = result + (both % 2) * bit
        bit *= 2
    return result


def kernel(
    n, q_hbm, k_hbm, v_hbm, g_hbm, o_ref, dq_ref, dk_ref, dv_ref,
    own, slots, raw, graw, stats, peak, total, accum, dq, dk, dv,
    load_sem, send_sem, recv_sem, relay_sem, stat_send, stat_recv,
):
    rows, width = q_hbm.shape
    factor = 1.0 / math.sqrt(width)
    scale = factor * math.log2(math.e)
    me = lax.axis_index("ctx")
    chips = n // 2
    chip, core = me // 2, me % 2
    sibling = chip * 2 + 1 - core
    Q, K, V, G = 0, 1, 2, 3

    loads = [
        pltpu.make_async_copy(src, own.at[i], load_sem.at[i])
        for i, src in enumerate((q_hbm, k_hbm, v_hbm, g_hbm))
    ]
    for load in loads:
        load.start()
    barrier = pltpu.get_barrier_semaphore()

    def greet(step, carry):
        other = (me + step) % n
        pl.semaphore_signal(barrier, inc=1, device_id={"ctx": other}, device_id_type=MESH)
        return carry

    lax.fori_loop(1, n, greet, 0)
    for load in loads:
        load.wait()
    pl.semaphore_wait(barrier, n - 1)

    def send_copy(part, other):
        above = (other > me).astype(jnp.int32)
        first = above * (K if part == 0 else V) + (1 - above) * (Q if part == 0 else G)
        return pltpu.make_async_remote_copy(
            src_ref=own.at[first],
            dst_ref=slots.at[me, part],
            send_sem=send_sem.at[other, part],
            recv_sem=recv_sem.at[me, part],
            device_id={"ctx": other},
            device_id_type=MESH,
        )

    def arrival(source, part):
        return pltpu.make_async_remote_copy(
            src_ref=slots.at[source, part],
            dst_ref=slots.at[source, part],
            send_sem=relay_sem.at[source, part],
            recv_sem=recv_sem.at[source, part],
            device_id={"ctx": sibling},
            device_id_type=MESH,
        )

    def send_all(step, carry):
        other = flip(chip, step, chips) * 2 + core
        send_copy(0, other).start()
        send_copy(1, other).start()
        return carry

    lax.fori_loop(1, chips, send_all, 0)
    send_copy(0, sibling).start()
    send_copy(1, sibling).start()

    def dot(a, b):
        return jnp.dot(a, b, preferred_element_type=jnp.float32)

    def dot_nt(a, b):
        return lax.dot_general(a, b, NT, preferred_element_type=jnp.float32)

    def fold(a):
        return sum(a[:, i : i + 128] for i in range(0, rows, 128))

    row = lax.broadcasted_iota(jnp.int32, (rows, rows), 0)
    col = lax.broadcasted_iota(jnp.int32, (rows, rows), 1)
    scores = jnp.where(col <= row, dot_nt(own[Q], own[K]) * scale, LOWEST)
    raw[me] = scores
    graw[me] = dot_nt(own[G], own[V])
    top = jnp.max(scores, axis=1, keepdims=True)
    probs = jnp.exp2(scores - top)
    peak[...] = jnp.broadcast_to(top, peak.shape)
    total[...] = fold(probs)
    accum[...] = dot(probs.astype(jnp.bfloat16), own[V])
    raw[n] = jnp.where(row <= col, dot_nt(own[K], own[Q]) * scale, LOWEST)
    graw[n] = dot_nt(own[V], own[G])

    def take(source):
        above = (source > me).astype(jnp.int32)
        left = own[above * K + (1 - above) * Q]
        right = own[above * V + (1 - above) * G]
        scores = dot_nt(left, slots[source, 0]) * scale
        raw[source] = scores
        graw[source] = dot_nt(right, slots[source, 1])

        @pl.when(source < me)
        def _():
            before = peak[...]
            s = raw[source]
            top = jnp.maximum(before, jnp.max(s, axis=1, keepdims=True))
            decay = jnp.exp2(before - top)
            probs = jnp.exp2(s - top[:, :1])
            peak[...] = top
            total[...] = total[...] * decay + fold(probs)
            accum[...] = accum[...] * decay[:, :1] + dot(
                probs.astype(jnp.bfloat16), slots[source, 1]
            )

    def stat_copy(source, other):
        return pltpu.make_async_remote_copy(
            src_ref=stats.at[source],
            dst_ref=stats.at[source],
            send_sem=stat_send.at[other],
            recv_sem=stat_recv.at[source],
            device_id={"ctx": other},
            device_id_type=MESH,
        )

    def send_stats(other, carry):
        stat_copy(me, other).start()
        return carry

    def finish_rows():
        ahead = jnp.sum(total[...], axis=1, keepdims=True)
        log_total = peak[:, :1] + jnp.log2(ahead)
        out = (accum[...] / ahead).astype(jnp.bfloat16)
        o_ref[...] = out
        product = own[G].astype(jnp.float32) * out.astype(jnp.float32)
        delta = jnp.sum(product, axis=1, keepdims=True)
        lane = lax.broadcasted_iota(jnp.int32, (rows, 128), 1)
        both = jnp.where(lane < 4, log_total, delta)
        stats[me] = jnp.transpose(both)[:8, :]
        lax.fori_loop(0, me, send_stats, 0)
        peak[...] = jnp.broadcast_to(log_total, peak.shape)
        total[...] = jnp.broadcast_to(delta, total.shape)

    last = 0
    bit = 1
    while bit < chips:
        last = last + bit * (chip >= bit).astype(jnp.int32)
        bit *= 2

    def receive(step, carry):
        far = flip(chip, step, chips) * 2

        @pl.when(step > 0)
        def _():
            for part in range(2):
                arrival(far + core, part).wait_recv()
                arrival(far + core, part).start()
            take(far + core)

        for part in range(2):
            arrival(far + 1 - core, part).wait_recv()
        take(far + 1 - core)

        @pl.when(step == last)
        def _():
            finish_rows()

        return carry

    lax.fori_loop(0, chips, receive, 0)

    def query_block(source, keys):
        probs = jnp.exp2(raw[source] - peak[:, :1])
        return dot((probs * (graw[source] - total[:, :1])).astype(jnp.bfloat16), keys)

    dq[...] = query_block(me, own[K])

    def query_step(source, carry):
        dq[...] += query_block(source, slots[source, 0])
        return carry

    lax.fori_loop(0, me, query_step, 0)
    dq_ref[...] = (dq[...] * factor).astype(jnp.bfloat16)

    def key_block(place, source, queries, grads):
        probs = jnp.exp2(raw[place] - stats[source, 0:1, :])
        gvalue = dot(probs.astype(jnp.bfloat16), grads)
        ds = (probs * (graw[place] - stats[source, 4:5, :])).astype(jnp.bfloat16)
        return dot(ds, queries), gvalue

    gk, gv = key_block(n, me, own[Q], own[G])
    dk[...] = gk
    dv[...] = gv

    def key_step(source, carry):
        stat_copy(source, sibling).wait_recv()
        gk, gv = key_block(source, source, slots[source, 0], slots[source, 1])
        dk[...] += gk
        dv[...] += gv
        return carry

    lax.fori_loop(me + 1, n, key_step, 0)
    dk_ref[...] = (dk[...] * factor).astype(jnp.bfloat16)
    dv_ref[...] = dv[...].astype(jnp.bfloat16)

    def drain(step, carry):
        far = flip(chip, step, chips) * 2 + core
        for part in range(2):
            send_copy(part, far).wait_send()
            arrival(far, part).wait_send()
        return carry

    lax.fori_loop(1, chips, drain, 0)
    for part in range(2):
        send_copy(part, sibling).wait_send()

    def drain_stats(other, carry):
        stat_copy(me, other).wait_send()
        return carry

    lax.fori_loop(0, me, drain_stats, 0)


def deliver(*refs):
    sources, targets, sem = refs[:4], refs[4:8], refs[8]
    copies = [
        pltpu.make_async_copy(source, target, sem.at[i])
        for i, (source, target) in enumerate(zip(sources, targets))
    ]
    for copy in copies:
        copy.start()
    for copy in copies:
        copy.wait()


def shards(n, queries, keys, values, grad_out):
    rows, width = queries.shape
    shape = jax.ShapeDtypeStruct((rows, width), jnp.bfloat16)
    f32 = jnp.float32
    results = pl.pallas_call(
        functools.partial(kernel, n),
        out_shape=(pltpu.VMEM((rows, width), jnp.bfloat16),) * 4,
        in_specs=[pl.BlockSpec(memory_space=pltpu.HBM)] * 4,
        out_specs=(pl.BlockSpec(memory_space=pltpu.VMEM),) * 4,
        scratch_shapes=[
            pltpu.VMEM((4, rows, width), jnp.bfloat16),
            pltpu.VMEM((n, 2, rows, width), jnp.bfloat16),
            pltpu.VMEM((n + 1, rows, rows), f32),
            pltpu.VMEM((n + 1, rows, rows), f32),
            pltpu.VMEM((n, 8, rows), f32),
            pltpu.VMEM((rows, 128), f32),
            pltpu.VMEM((rows, 128), f32),
            pltpu.VMEM((rows, width), f32),
            pltpu.VMEM((rows, width), f32),
            pltpu.VMEM((rows, width), f32),
            pltpu.VMEM((rows, width), f32),
            pltpu.SemaphoreType.DMA((4,)),
            pltpu.SemaphoreType.DMA((n, 2)),
            pltpu.SemaphoreType.DMA((n, 2)),
            pltpu.SemaphoreType.DMA((n, 2)),
            pltpu.SemaphoreType.DMA((n,)),
            pltpu.SemaphoreType.DMA((n,)),
        ],
        compiler_params=pltpu.CompilerParams(
            collective_id=0,
            has_side_effects=True,
            vmem_limit_bytes=60 * 1024 * 1024,
        ),
    )(queries, keys, values, grad_out)
    return pl.pallas_call(
        deliver,
        out_shape=(shape,) * 4,
        in_specs=[pl.BlockSpec(memory_space=pltpu.VMEM)] * 4,
        out_specs=(pl.BlockSpec(memory_space=pltpu.HBM),) * 4,
        scratch_shapes=[pltpu.SemaphoreType.DMA((4,))],
    )(*results)


def solution(mesh):
    placed = P(("grp", "ctx"), None)
    return jax.shard_map(
        functools.partial(shards, mesh.shape["ctx"]),
        mesh=mesh,
        in_specs=(placed,) * 4,
        out_specs=(placed,) * 4,
        check_vma=False,
    )
```

```python
import functools
import math

import jax
import jax.numpy as jnp
from jax import lax
from jax.experimental import pallas as pl
from jax.experimental.pallas import tpu as pltpu
from jax.sharding import PartitionSpec as P

MESH = pl.DeviceIdType.MESH
LOWEST = -1e30
NT = (((1,), (1,)), ((), ()))


def flip(index, by, count):
    result = 0
    bit = 1
    while bit < count:
        both = (index // bit) % 2 + (by // bit) % 2
        result = result + (both % 2) * bit
        bit *= 2
    return result


def kernel(
    n, q_hbm, k_hbm, v_hbm, g_hbm, o_ref, dq_ref, dk_ref, dv_ref,
    own, slots, raw, graw, stats, peak, total, accum, dq, dk, dv,
    load_sem, send_sem, recv_sem, relay_sem, stat_send, stat_recv,
):
    rows, width = q_hbm.shape
    factor = 1.0 / math.sqrt(width)
    scale = factor * math.log2(math.e)
    me = lax.axis_index("ctx")
    chips = n // 2
    chip, core = me // 2, me % 2
    sibling = chip * 2 + 1 - core
    Q, K, V, G = 0, 1, 2, 3

    loads = [
        pltpu.make_async_copy(src, own.at[i], load_sem.at[i])
        for i, src in enumerate((q_hbm, k_hbm, v_hbm, g_hbm))
    ]
    for load in loads:
        load.start()
    barrier = pltpu.get_barrier_semaphore()

    def greet(step, carry):
        other = (me + step) % n
        pl.semaphore_signal(barrier, inc=1, device_id={"ctx": other}, device_id_type=MESH)
        return carry

    lax.fori_loop(1, n, greet, 0)
    for load in loads:
        load.wait()
    pl.semaphore_wait(barrier, n - 1)

    def send_copy(part, other):
        above = (other > me).astype(jnp.int32)
        first = above * (K if part == 0 else V) + (1 - above) * (Q if part == 0 else G)
        return pltpu.make_async_remote_copy(
            src_ref=own.at[first],
            dst_ref=slots.at[me, part],
            send_sem=send_sem.at[other, part],
            recv_sem=recv_sem.at[me, part],
            device_id={"ctx": other},
            device_id_type=MESH,
        )

    def arrival(source, part):
        return pltpu.make_async_remote_copy(
            src_ref=slots.at[source, part],
            dst_ref=slots.at[source, part],
            send_sem=relay_sem.at[source, part],
            recv_sem=recv_sem.at[source, part],
            device_id={"ctx": sibling},
            device_id_type=MESH,
        )

    def send_all(step, carry):
        other = flip(chip, step, chips) * 2 + core
        send_copy(0, other).start()
        send_copy(1, other).start()
        return carry

    lax.fori_loop(1, chips, send_all, 0)
    send_copy(0, sibling).start()
    send_copy(1, sibling).start()

    def dot(a, b):
        return jnp.dot(a, b, preferred_element_type=jnp.float32)

    def dot_nt(a, b):
        return lax.dot_general(a, b, NT, preferred_element_type=jnp.float32)

    def fold(a):
        return sum(a[:, i : i + 128] for i in range(0, rows, 128))

    def wide(a):
        return jnp.concatenate([a] * (rows // 128), axis=1)

    row = lax.broadcasted_iota(jnp.int32, (rows, rows), 0)
    col = lax.broadcasted_iota(jnp.int32, (rows, rows), 1)
    scores = jnp.where(col <= row, dot_nt(own[Q], own[K]) * scale, LOWEST)
    raw[me] = scores
    graw[me] = dot_nt(own[G], own[V])
    top = jnp.max(scores, axis=1, keepdims=True)
    probs = jnp.exp2(scores - top)
    peak[...] = jnp.broadcast_to(top, peak.shape)
    total[...] = fold(probs)
    accum[...] = dot(probs.astype(jnp.bfloat16), own[V])
    raw[n] = jnp.where(row <= col, dot_nt(own[K], own[Q]) * scale, LOWEST)
    graw[n] = dot_nt(own[V], own[G])

    def take(source):
        above = (source > me).astype(jnp.int32)
        left = own[above * K + (1 - above) * Q]
        right = own[above * V + (1 - above) * G]
        scores = dot_nt(left, slots[source, 0]) * scale
        raw[source] = scores
        graw[source] = dot_nt(right, slots[source, 1])

        @pl.when(source < me)
        def _():
            before = peak[...]
            s = raw[source]
            top = jnp.maximum(before, jnp.max(s, axis=1, keepdims=True))
            decay = jnp.exp2(before - top)
            probs = jnp.exp2(s - wide(top))
            peak[...] = top
            total[...] = total[...] * decay + fold(probs)
            accum[...] = accum[...] * decay + dot(
                probs.astype(jnp.bfloat16), slots[source, 1]
            )

    def stat_copy(source, other):
        return pltpu.make_async_remote_copy(
            src_ref=stats.at[source],
            dst_ref=stats.at[source],
            send_sem=stat_send.at[other],
            recv_sem=stat_recv.at[source],
            device_id={"ctx": other},
            device_id_type=MESH,
        )

    def send_stats(other, carry):
        stat_copy(me, other).start()
        return carry

    def finish_rows():
        ahead = jnp.sum(total[...], axis=1, keepdims=True)
        log_total = peak[:, :1] + jnp.log2(ahead)
        out = (accum[...] / ahead).astype(jnp.bfloat16)
        o_ref[...] = out
        product = own[G].astype(jnp.float32) * out.astype(jnp.float32)
        delta = jnp.sum(product, axis=1, keepdims=True)
        lane = lax.broadcasted_iota(jnp.int32, (rows, 128), 1)
        both = jnp.where(lane < 4, log_total, delta)
        stats[me] = jnp.transpose(both)[:8, :]
        lax.fori_loop(0, me, send_stats, 0)
        peak[...] = jnp.broadcast_to(log_total, peak.shape)
        total[...] = jnp.broadcast_to(delta, total.shape)

    last = 0
    bit = 1
    while bit < chips:
        last = last + bit * (chip >= bit).astype(jnp.int32)
        bit *= 2

    def receive(step, carry):
        far = flip(chip, step, chips) * 2

        @pl.when(step > 0)
        def _():
            for part in range(2):
                arrival(far + core, part).wait_recv()
                arrival(far + core, part).start()
            take(far + core)

        for part in range(2):
            arrival(far + 1 - core, part).wait_recv()
        take(far + 1 - core)

        @pl.when(step == last)
        def _():
            finish_rows()

        return carry

    lax.fori_loop(0, chips, receive, 0)

    def query_block(source, keys):
        probs = jnp.exp2(raw[source] - wide(peak[...]))
        return dot((probs * (graw[source] - wide(total[...]))).astype(jnp.bfloat16), keys)

    dq[...] = query_block(me, own[K])

    def query_step(source, carry):
        dq[...] += query_block(source, slots[source, 0])
        return carry

    lax.fori_loop(0, me, query_step, 0)
    dq_ref[...] = (dq[...] * factor).astype(jnp.bfloat16)

    def key_block(place, source, queries, grads):
        probs = jnp.exp2(raw[place] - stats[source, 0:1, :])
        gvalue = dot(probs.astype(jnp.bfloat16), grads)
        ds = (probs * (graw[place] - stats[source, 4:5, :])).astype(jnp.bfloat16)
        return dot(ds, queries), gvalue

    gk, gv = key_block(n, me, own[Q], own[G])
    dk[...] = gk
    dv[...] = gv

    def key_step(source, carry):
        stat_copy(source, sibling).wait_recv()
        gk, gv = key_block(source, source, slots[source, 0], slots[source, 1])
        dk[...] += gk
        dv[...] += gv
        return carry

    lax.fori_loop(me + 1, n, key_step, 0)
    dk_ref[...] = (dk[...] * factor).astype(jnp.bfloat16)
    dv_ref[...] = dv[...].astype(jnp.bfloat16)

    def drain(step, carry):
        far = flip(chip, step, chips) * 2 + core
        for part in range(2):
            send_copy(part, far).wait_send()
            arrival(far, part).wait_send()
        return carry

    lax.fori_loop(1, chips, drain, 0)
    for part in range(2):
        send_copy(part, sibling).wait_send()

    def drain_stats(other, carry):
        stat_copy(me, other).wait_send()
        return carry

    lax.fori_loop(0, me, drain_stats, 0)


def deliver(*refs):
    sources, targets, sem = refs[:4], refs[4:8], refs[8]
    copies = [
        pltpu.make_async_copy(source, target, sem.at[i])
        for i, (source, target) in enumerate(zip(sources, targets))
    ]
    for copy in copies:
        copy.start()
    for copy in copies:
        copy.wait()


def shards(n, queries, keys, values, grad_out):
    rows, width = queries.shape
    shape = jax.ShapeDtypeStruct((rows, width), jnp.bfloat16)
    f32 = jnp.float32
    results = pl.pallas_call(
        functools.partial(kernel, n),
        out_shape=(pltpu.VMEM((rows, width), jnp.bfloat16),) * 4,
        in_specs=[pl.BlockSpec(memory_space=pltpu.HBM)] * 4,
        out_specs=(pl.BlockSpec(memory_space=pltpu.VMEM),) * 4,
        scratch_shapes=[
            pltpu.VMEM((4, rows, width), jnp.bfloat16),
            pltpu.VMEM((n, 2, rows, width), jnp.bfloat16),
            pltpu.VMEM((n + 1, rows, rows), f32),
            pltpu.VMEM((n + 1, rows, rows), f32),
            pltpu.VMEM((n, 8, rows), f32),
            pltpu.VMEM((rows, 128), f32),
            pltpu.VMEM((rows, 128), f32),
            pltpu.VMEM((rows, width), f32),
            pltpu.VMEM((rows, width), f32),
            pltpu.VMEM((rows, width), f32),
            pltpu.VMEM((rows, width), f32),
            pltpu.SemaphoreType.DMA((4,)),
            pltpu.SemaphoreType.DMA((n, 2)),
            pltpu.SemaphoreType.DMA((n, 2)),
            pltpu.SemaphoreType.DMA((n, 2)),
            pltpu.SemaphoreType.DMA((n,)),
            pltpu.SemaphoreType.DMA((n,)),
        ],
        compiler_params=pltpu.CompilerParams(
            collective_id=0,
            has_side_effects=True,
            vmem_limit_bytes=60 * 1024 * 1024,
        ),
    )(queries, keys, values, grad_out)
    return pl.pallas_call(
        deliver,
        out_shape=(shape,) * 4,
        in_specs=[pl.BlockSpec(memory_space=pltpu.VMEM)] * 4,
        out_specs=(pl.BlockSpec(memory_space=pltpu.HBM),) * 4,
        scratch_shapes=[pltpu.SemaphoreType.DMA((4,))],
        compiler_params=pltpu.CompilerParams(vmem_limit_bytes=2 * 1024 * 1024),
    )(*results)


def solution(mesh):
    placed = P(("grp", "ctx"), None)
    return jax.shard_map(
        functools.partial(shards, mesh.shape["ctx"]),
        mesh=mesh,
        in_specs=(placed,) * 4,
        out_specs=(placed,) * 4,
        check_vma=False,
    )
```

```python
import functools
import math

import jax
import jax.numpy as jnp
from jax import lax
from jax.experimental import pallas as pl
from jax.experimental.pallas import tpu as pltpu
from jax.sharding import PartitionSpec as P

MESH = pl.DeviceIdType.MESH
LOWEST = -1e30
NT = (((1,), (1,)), ((), ()))


def flip(index, by, count):
    result = 0
    bit = 1
    while bit < count:
        both = (index // bit) % 2 + (by // bit) % 2
        result = result + (both % 2) * bit
        bit *= 2
    return result


def kernel(
    n, q_hbm, k_hbm, v_hbm, g_hbm, o_ref, dq_ref, dk_ref, dv_ref,
    own, slots, raw, graw, stats, peak, total, accum, dq, dk, dv,
    load_sem, send_sem, recv_sem, relay_sem, onward_sem, forward_sem, stat_send, stat_recv,
):
    rows, width = q_hbm.shape
    factor = 1.0 / math.sqrt(width)
    scale = factor * math.log2(math.e)
    me = lax.axis_index("ctx")
    chips = n // 2
    chip, core = me // 2, me % 2
    sibling = chip * 2 + 1 - core
    Q, K, V, G = 0, 1, 2, 3

    loads = [
        pltpu.make_async_copy(src, own.at[i], load_sem.at[i])
        for i, src in enumerate((q_hbm, k_hbm, v_hbm, g_hbm))
    ]
    for load in loads:
        load.start()
    barrier = pltpu.get_barrier_semaphore()

    def greet(step, carry):
        other = (me + step) % n
        pl.semaphore_signal(barrier, inc=1, device_id={"ctx": other}, device_id_type=MESH)
        return carry

    square = chips == 4
    if square:
        across = flip(chip, 3, chips) * 2 + core
        for other in (sibling, flip(chip, 1, 4) * 2 + core, flip(chip, 2, 4) * 2 + core):
            pl.semaphore_signal(barrier, inc=1, device_id={"ctx": other}, device_id_type=MESH)

        @pl.when(chip != 3)
        def _():
            pl.semaphore_signal(barrier, inc=1, device_id={"ctx": across}, device_id_type=MESH)

        for load in loads:
            load.wait()
        pl.semaphore_wait(barrier, 3 + (chip != 0).astype(jnp.int32))

        @pl.when(chip == 1)
        def _():
            pl.semaphore_signal(onward_sem, inc=1, device_id={"ctx": core}, device_id_type=MESH)

    else:
        lax.fori_loop(1, n, greet, 0)
        for load in loads:
            load.wait()
        pl.semaphore_wait(barrier, n - 1)

    def send_copy(part, other):
        above = (other > me).astype(jnp.int32)
        first = above * (K if part == 0 else V) + (1 - above) * (Q if part == 0 else G)
        return pltpu.make_async_remote_copy(
            src_ref=own.at[first],
            dst_ref=slots.at[me, part],
            send_sem=send_sem.at[other, part],
            recv_sem=recv_sem.at[me, part],
            device_id={"ctx": other},
            device_id_type=MESH,
        )

    def arrival(source, part):
        return pltpu.make_async_remote_copy(
            src_ref=slots.at[source, part],
            dst_ref=slots.at[source, part],
            send_sem=relay_sem.at[source, part],
            recv_sem=recv_sem.at[source, part],
            device_id={"ctx": sibling},
            device_id_type=MESH,
        )

    def send_all(step, carry):
        other = flip(chip, step, chips) * 2 + core
        send_copy(0, other).start()
        send_copy(1, other).start()
        return carry

    def forward():
        return pltpu.make_async_remote_copy(
            src_ref=slots.at[core, 1],
            dst_ref=slots.at[core, 1],
            send_sem=forward_sem,
            recv_sem=recv_sem.at[core, 1],
            device_id={"ctx": 6 + core},
            device_id_type=MESH,
        )

    def send_to(*copies):
        for part, other in copies:
            send_copy(part, other * 2 + core).start()

    def send_sibling():
        send_copy(0, sibling).start()
        send_copy(1, sibling).start()

    if square:

        @pl.when(chip == 0)
        def _():
            send_to((0, 1), (1, 1), (0, 2), (1, 2))
            send_sibling()

        @pl.when(chip == 1)
        def _():
            send_to((0, 0), (1, 0), (0, 3), (1, 3), (0, 2), (1, 2))
            send_sibling()

        @pl.when(chip == 2)
        def _():
            send_to((0, 3), (1, 3), (0, 0), (1, 0))
            send_sibling()

        @pl.when(chip == 3)
        def _():
            send_to((0, 2), (1, 2), (0, 1), (1, 1), (0, 0), (1, 0))
            send_sibling()

    else:
        lax.fori_loop(1, chips, send_all, 0)
        send_sibling()

    def dot(a, b):
        return jnp.dot(a, b, preferred_element_type=jnp.float32)

    def dot_nt(a, b):
        return lax.dot_general(a, b, NT, preferred_element_type=jnp.float32)

    def fold(a):
        return sum(a[:, i : i + 128] for i in range(0, rows, 128))

    def wide(a):
        return jnp.concatenate([a] * (rows // 128), axis=1)

    row = lax.broadcasted_iota(jnp.int32, (rows, rows), 0)
    col = lax.broadcasted_iota(jnp.int32, (rows, rows), 1)
    scores = jnp.where(col <= row, dot_nt(own[Q], own[K]) * scale, LOWEST)
    raw[me] = scores
    graw[me] = dot_nt(own[G], own[V])
    top = jnp.max(scores, axis=1, keepdims=True)
    probs = jnp.exp2(scores - top)
    peak[...] = jnp.broadcast_to(top, peak.shape)
    total[...] = fold(probs)
    accum[...] = dot(probs.astype(jnp.bfloat16), own[V])
    raw[n] = jnp.where(row <= col, dot_nt(own[K], own[Q]) * scale, LOWEST)
    graw[n] = dot_nt(own[V], own[G])
    if square:

        @pl.when(chip == 0)
        def _():
            pl.semaphore_wait(onward_sem, 1)
            send_to((0, 3))

        @pl.when(chip == 2)
        def _():
            arrival(core, 1).wait_recv()
            forward().start()
            arrival(core, 1).start()
            send_to((0, 1), (1, 1))


    def take(source):
        above = (source > me).astype(jnp.int32)
        left = own[above * K + (1 - above) * Q]
        right = own[above * V + (1 - above) * G]
        scores = dot_nt(left, slots[source, 0]) * scale
        raw[source] = scores
        graw[source] = dot_nt(right, slots[source, 1])

        @pl.when(source < me)
        def _():
            before = peak[...]
            s = raw[source]
            top = jnp.maximum(before, jnp.max(s, axis=1, keepdims=True))
            decay = jnp.exp2(before - top)
            probs = jnp.exp2(s - wide(top))
            peak[...] = top
            total[...] = total[...] * decay + fold(probs)
            accum[...] = accum[...] * decay + dot(
                probs.astype(jnp.bfloat16), slots[source, 1]
            )

    def stat_copy(source, other):
        return pltpu.make_async_remote_copy(
            src_ref=stats.at[source],
            dst_ref=stats.at[source],
            send_sem=stat_send.at[other],
            recv_sem=stat_recv.at[source],
            device_id={"ctx": other},
            device_id_type=MESH,
        )

    def send_stats(other, carry):
        stat_copy(me, other).start()
        return carry

    def finish_rows():
        ahead = jnp.sum(total[...], axis=1, keepdims=True)
        log_total = peak[:, :1] + jnp.log2(ahead)
        out = (accum[...] / ahead).astype(jnp.bfloat16)
        o_ref[...] = out
        product = own[G].astype(jnp.float32) * out.astype(jnp.float32)
        delta = jnp.sum(product, axis=1, keepdims=True)
        lane = lax.broadcasted_iota(jnp.int32, (rows, 128), 1)
        both = jnp.where(lane < 4, log_total, delta)
        stats[me] = jnp.transpose(both)[:8, :]
        lax.fori_loop(0, me, send_stats, 0)
        peak[...] = jnp.broadcast_to(log_total, peak.shape)
        total[...] = jnp.broadcast_to(delta, total.shape)

    last = 0
    bit = 1
    while bit < chips:
        last = last + bit * (chip >= bit).astype(jnp.int32)
        bit *= 2

    def receive(event, carry):
        step = event
        if square:
            step = event + ((event == 1).astype(jnp.int32) - (event == 2).astype(jnp.int32)) * (
                1 - chip % 2
            )
        far = flip(chip, step, chips) * 2

        @pl.when(step > 0)
        def _():
            arrival(far + core, 0).wait_recv()
            arrival(far + core, 0).start()
            handled = square & (chip == 2) & (step == 2)

            @pl.when(jnp.logical_not(handled))
            def _():
                arrival(far + core, 1).wait_recv()
                arrival(far + core, 1).start()

            take(far + core)

        for part in range(2):
            arrival(far + 1 - core, part).wait_recv()
        take(far + 1 - core)

        @pl.when(event == last)
        def _():
            finish_rows()

        return carry

    lax.fori_loop(0, chips, receive, 0)

    def query_block(source, keys):
        probs = jnp.exp2(raw[source] - wide(peak[...]))
        return dot((probs * (graw[source] - wide(total[...]))).astype(jnp.bfloat16), keys)

    dq[...] = query_block(me, own[K])

    def query_step(source, carry):
        dq[...] += query_block(source, slots[source, 0])
        return carry

    lax.fori_loop(0, me, query_step, 0)
    dq_ref[...] = (dq[...] * factor).astype(jnp.bfloat16)

    def key_block(place, source, queries, grads):
        probs = jnp.exp2(raw[place] - stats[source, 0:1, :])
        gvalue = dot(probs.astype(jnp.bfloat16), grads)
        ds = (probs * (graw[place] - stats[source, 4:5, :])).astype(jnp.bfloat16)
        return dot(ds, queries), gvalue

    gk, gv = key_block(n, me, own[Q], own[G])
    dk[...] = gk
    dv[...] = gv

    def key_step(source, carry):
        stat_copy(source, sibling).wait_recv()
        gk, gv = key_block(source, source, slots[source, 0], slots[source, 1])
        dk[...] += gk
        dv[...] += gv
        return carry

    lax.fori_loop(me + 1, n, key_step, 0)
    dk_ref[...] = (dk[...] * factor).astype(jnp.bfloat16)
    dv_ref[...] = dv[...].astype(jnp.bfloat16)

    def drain(step, carry):
        far = flip(chip, step, chips) * 2 + core
        for part in range(2):
            arrival(far, part).wait_send()
        send_copy(0, far).wait_send()

        @pl.when(jnp.logical_not(square & (chip == 0) & (step == 3)))
        def _():
            send_copy(1, far).wait_send()

        return carry

    lax.fori_loop(1, chips, drain, 0)
    if square:

        @pl.when(chip == 2)
        def _():
            forward().wait_send()

    for part in range(2):
        send_copy(part, sibling).wait_send()

    def drain_stats(other, carry):
        stat_copy(me, other).wait_send()
        return carry

    lax.fori_loop(0, me, drain_stats, 0)


def deliver(*refs):
    sources, targets, sem = refs[:4], refs[4:8], refs[8]
    copies = [
        pltpu.make_async_copy(source, target, sem.at[i])
        for i, (source, target) in enumerate(zip(sources, targets))
    ]
    for copy in copies:
        copy.start()
    for copy in copies:
        copy.wait()


def shards(n, queries, keys, values, grad_out):
    rows, width = queries.shape
    shape = jax.ShapeDtypeStruct((rows, width), jnp.bfloat16)
    f32 = jnp.float32
    results = pl.pallas_call(
        functools.partial(kernel, n),
        out_shape=(pltpu.VMEM((rows, width), jnp.bfloat16),) * 4,
        in_specs=[pl.BlockSpec(memory_space=pltpu.HBM)] * 4,
        out_specs=(pl.BlockSpec(memory_space=pltpu.VMEM),) * 4,
        scratch_shapes=[
            pltpu.VMEM((4, rows, width), jnp.bfloat16),
            pltpu.VMEM((n, 2, rows, width), jnp.bfloat16),
            pltpu.VMEM((n + 1, rows, rows), f32),
            pltpu.VMEM((n + 1, rows, rows), f32),
            pltpu.VMEM((n, 8, rows), f32),
            pltpu.VMEM((rows, 128), f32),
            pltpu.VMEM((rows, 128), f32),
            pltpu.VMEM((rows, width), f32),
            pltpu.VMEM((rows, width), f32),
            pltpu.VMEM((rows, width), f32),
            pltpu.VMEM((rows, width), f32),
            pltpu.SemaphoreType.DMA((4,)),
            pltpu.SemaphoreType.DMA((n, 2)),
            pltpu.SemaphoreType.DMA((n, 2)),
            pltpu.SemaphoreType.DMA((n, 2)),
            pltpu.SemaphoreType.REGULAR,
            pltpu.SemaphoreType.DMA,
            pltpu.SemaphoreType.DMA((n,)),
            pltpu.SemaphoreType.DMA((n,)),
        ],
        compiler_params=pltpu.CompilerParams(
            collective_id=0,
            has_side_effects=True,
            vmem_limit_bytes=60 * 1024 * 1024,
        ),
    )(queries, keys, values, grad_out)
    return pl.pallas_call(
        deliver,
        out_shape=(shape,) * 4,
        in_specs=[pl.BlockSpec(memory_space=pltpu.VMEM)] * 4,
        out_specs=(pl.BlockSpec(memory_space=pltpu.HBM),) * 4,
        scratch_shapes=[pltpu.SemaphoreType.DMA((4,))],
        compiler_params=pltpu.CompilerParams(vmem_limit_bytes=2 * 1024 * 1024),
    )(*results)


def solution(mesh):
    placed = P(("grp", "ctx"), None)
    return jax.shard_map(
        functools.partial(shards, mesh.shape["ctx"]),
        mesh=mesh,
        in_specs=(placed,) * 4,
        out_specs=(placed,) * 4,
        check_vma=False,
    )
```

```python
import functools
import math

import jax
import jax.numpy as jnp
from jax import lax
from jax.experimental import pallas as pl
from jax.experimental.pallas import tpu as pltpu
from jax.sharding import PartitionSpec as P

MESH = pl.DeviceIdType.MESH
LOWEST = -1e30
NT = (((1,), (1,)), ((), ()))


def flip(index, by, count):
    result = 0
    bit = 1
    while bit < count:
        both = (index // bit) % 2 + (by // bit) % 2
        result = result + (both % 2) * bit
        bit *= 2
    return result


def kernel(
    n, q_hbm, k_hbm, v_hbm, g_hbm, o_ref, dq_ref, dk_ref, dv_ref,
    own, slots, raw, graw, stats, peak, total, accum, dq, dk, dv,
    load_sem, send_sem, recv_sem, relay_sem, onward_sem, forward_sem, stat_send, stat_recv,
):
    rows, width = q_hbm.shape
    factor = 1.0 / math.sqrt(width)
    scale = factor * math.log2(math.e)
    me = lax.axis_index("ctx")
    chips = n // 2
    chip, core = me // 2, me % 2
    sibling = chip * 2 + 1 - core
    Q, K, V, G = 0, 1, 2, 3

    loads = [
        pltpu.make_async_copy(src, own.at[i], load_sem.at[i])
        for i, src in enumerate((q_hbm, k_hbm, v_hbm, g_hbm))
    ]
    for load in loads:
        load.start()
    barrier = pltpu.get_barrier_semaphore()

    def greet(step, carry):
        other = (me + step) % n
        pl.semaphore_signal(barrier, inc=1, device_id={"ctx": other}, device_id_type=MESH)
        return carry

    square = chips == 4
    if square:
        across = flip(chip, 3, chips) * 2 + core
        for other in (sibling, flip(chip, 1, 4) * 2 + core, flip(chip, 2, 4) * 2 + core):
            pl.semaphore_signal(barrier, inc=1, device_id={"ctx": other}, device_id_type=MESH)

        @pl.when(chip != 3)
        def _():
            pl.semaphore_signal(barrier, inc=1, device_id={"ctx": across}, device_id_type=MESH)

        for load in loads:
            load.wait()
        pl.semaphore_wait(barrier, 3 + (chip != 0).astype(jnp.int32))

        @pl.when(chip == 1)
        def _():
            pl.semaphore_signal(onward_sem, inc=1, device_id={"ctx": core}, device_id_type=MESH)

    else:
        lax.fori_loop(1, n, greet, 0)
        for load in loads:
            load.wait()
        pl.semaphore_wait(barrier, n - 1)

    def send_copy(part, other):
        above = (other > me).astype(jnp.int32)
        first = above * (K if part == 0 else V) + (1 - above) * (Q if part == 0 else G)
        return pltpu.make_async_remote_copy(
            src_ref=own.at[first],
            dst_ref=slots.at[me, part],
            send_sem=send_sem.at[other, part],
            recv_sem=recv_sem.at[me, part],
            device_id={"ctx": other},
            device_id_type=MESH,
        )

    def arrival(source, part):
        return pltpu.make_async_remote_copy(
            src_ref=slots.at[source, part],
            dst_ref=slots.at[source, part],
            send_sem=relay_sem.at[source, part],
            recv_sem=recv_sem.at[source, part],
            device_id={"ctx": sibling},
            device_id_type=MESH,
        )

    def send_all(step, carry):
        other = flip(chip, step, chips) * 2 + core
        send_copy(0, other).start()
        send_copy(1, other).start()
        return carry

    def forward():
        return pltpu.make_async_remote_copy(
            src_ref=slots.at[core, 1],
            dst_ref=slots.at[core, 1],
            send_sem=forward_sem,
            recv_sem=recv_sem.at[core, 1],
            device_id={"ctx": 6 + core},
            device_id_type=MESH,
        )

    def send_to(*copies):
        for part, other in copies:
            send_copy(part, other * 2 + core).start()

    def send_sibling():
        send_copy(0, sibling).start()
        send_copy(1, sibling).start()

    if square:

        @pl.when(chip == 0)
        def _():
            send_to((0, 2), (1, 2), (0, 1), (1, 1))
            send_sibling()

        @pl.when(chip == 1)
        def _():
            send_to((0, 0), (1, 0), (0, 3), (1, 3), (0, 2), (1, 2))
            send_sibling()

        @pl.when(chip == 2)
        def _():
            send_to((0, 3), (1, 3), (0, 0), (1, 0))
            send_sibling()

        @pl.when(chip == 3)
        def _():
            send_to((0, 2), (1, 2), (0, 1), (1, 1), (0, 0), (1, 0))
            send_sibling()

    else:
        lax.fori_loop(1, chips, send_all, 0)
        send_sibling()

    def dot(a, b):
        return jnp.dot(a, b, preferred_element_type=jnp.float32)

    def dot_nt(a, b):
        return lax.dot_general(a, b, NT, preferred_element_type=jnp.float32)

    def fold(a):
        return sum(a[:, i : i + 128] for i in range(0, rows, 128))

    def wide(a):
        return jnp.concatenate([a] * (rows // 128), axis=1)

    row = lax.broadcasted_iota(jnp.int32, (rows, rows), 0)
    col = lax.broadcasted_iota(jnp.int32, (rows, rows), 1)
    scores = jnp.where(col <= row, dot_nt(own[Q], own[K]) * scale, LOWEST)
    raw[me] = scores
    graw[me] = dot_nt(own[G], own[V])
    top = jnp.max(scores, axis=1, keepdims=True)
    probs = jnp.exp2(scores - top)
    peak[...] = jnp.broadcast_to(top, peak.shape)
    total[...] = fold(probs)
    accum[...] = dot(probs.astype(jnp.bfloat16), own[V])
    raw[n] = jnp.where(row <= col, dot_nt(own[K], own[Q]) * scale, LOWEST)
    graw[n] = dot_nt(own[V], own[G])
    if square:

        @pl.when(chip == 0)
        def _():
            pl.semaphore_wait(onward_sem, 1)
            send_to((0, 3))

        @pl.when(chip == 2)
        def _():
            arrival(core, 1).wait_recv()
            forward().start()
            arrival(core, 1).start()
            send_to((0, 1), (1, 1))


    def take(source):
        above = (source > me).astype(jnp.int32)
        left = own[above * K + (1 - above) * Q]
        right = own[above * V + (1 - above) * G]
        scores = dot_nt(left, slots[source, 0]) * scale
        raw[source] = scores
        graw[source] = dot_nt(right, slots[source, 1])

        @pl.when(source < me)
        def _():
            before = peak[...]
            s = raw[source]
            top = jnp.maximum(before, jnp.max(s, axis=1, keepdims=True))
            decay = jnp.exp2(before - top)
            probs = jnp.exp2(s - wide(top))
            peak[...] = top
            total[...] = total[...] * decay + fold(probs)
            accum[...] = accum[...] * decay + dot(
                probs.astype(jnp.bfloat16), slots[source, 1]
            )

    def stat_copy(source, other):
        return pltpu.make_async_remote_copy(
            src_ref=stats.at[source],
            dst_ref=stats.at[source],
            send_sem=stat_send.at[other],
            recv_sem=stat_recv.at[source],
            device_id={"ctx": other},
            device_id_type=MESH,
        )

    def send_stats(other, carry):
        stat_copy(me, other).start()
        return carry

    def finish_rows():
        ahead = jnp.sum(total[...], axis=1, keepdims=True)
        log_total = peak[:, :1] + jnp.log2(ahead)
        out = (accum[...] / ahead).astype(jnp.bfloat16)
        o_ref[...] = out
        product = own[G].astype(jnp.float32) * out.astype(jnp.float32)
        delta = jnp.sum(product, axis=1, keepdims=True)
        lane = lax.broadcasted_iota(jnp.int32, (rows, 128), 1)
        both = jnp.where(lane < 4, log_total, delta)
        stats[me] = jnp.transpose(both)[:8, :]
        lax.fori_loop(0, me, send_stats, 0)
        peak[...] = jnp.broadcast_to(log_total, peak.shape)
        total[...] = jnp.broadcast_to(delta, total.shape)

    last = 0
    bit = 1
    while bit < chips:
        last = last + bit * (chip >= bit).astype(jnp.int32)
        bit *= 2

    def receive(event, carry):
        step = event
        if square:
            step = event + ((event == 1).astype(jnp.int32) - (event == 2).astype(jnp.int32)) * (
                1 - chip % 2
            )
        far = flip(chip, step, chips) * 2

        @pl.when(step > 0)
        def _():
            arrival(far + core, 0).wait_recv()
            arrival(far + core, 0).start()
            handled = square & (chip == 2) & (step == 2)

            @pl.when(jnp.logical_not(handled))
            def _():
                arrival(far + core, 1).wait_recv()
                arrival(far + core, 1).start()

            take(far + core)

        for part in range(2):
            arrival(far + 1 - core, part).wait_recv()
        take(far + 1 - core)

        @pl.when(event == last)
        def _():
            finish_rows()

        return carry

    lax.fori_loop(0, chips, receive, 0)

    def query_block(source, keys):
        probs = jnp.exp2(raw[source] - wide(peak[...]))
        return dot((probs * (graw[source] - wide(total[...]))).astype(jnp.bfloat16), keys)

    dq[...] = query_block(me, own[K])

    def query_step(source, carry):
        dq[...] += query_block(source, slots[source, 0])
        return carry

    lax.fori_loop(0, me, query_step, 0)
    dq_ref[...] = (dq[...] * factor).astype(jnp.bfloat16)

    def key_block(place, source, queries, grads):
        probs = jnp.exp2(raw[place] - stats[source, 0:1, :])
        gvalue = dot(probs.astype(jnp.bfloat16), grads)
        ds = (probs * (graw[place] - stats[source, 4:5, :])).astype(jnp.bfloat16)
        return dot(ds, queries), gvalue

    gk, gv = key_block(n, me, own[Q], own[G])
    dk[...] = gk
    dv[...] = gv

    def key_step(source, carry):
        stat_copy(source, sibling).wait_recv()
        gk, gv = key_block(source, source, slots[source, 0], slots[source, 1])
        dk[...] += gk
        dv[...] += gv
        return carry

    lax.fori_loop(me + 1, n, key_step, 0)
    dk_ref[...] = (dk[...] * factor).astype(jnp.bfloat16)
    dv_ref[...] = dv[...].astype(jnp.bfloat16)

    def drain(step, carry):
        far = flip(chip, step, chips) * 2 + core
        for part in range(2):
            arrival(far, part).wait_send()
        send_copy(0, far).wait_send()

        @pl.when(jnp.logical_not(square & (chip == 0) & (step == 3)))
        def _():
            send_copy(1, far).wait_send()

        return carry

    lax.fori_loop(1, chips, drain, 0)
    if square:

        @pl.when(chip == 2)
        def _():
            forward().wait_send()

    for part in range(2):
        send_copy(part, sibling).wait_send()

    def drain_stats(other, carry):
        stat_copy(me, other).wait_send()
        return carry

    lax.fori_loop(0, me, drain_stats, 0)


def deliver(*refs):
    sources, targets, sem = refs[:4], refs[4:8], refs[8]
    copies = [
        pltpu.make_async_copy(source, target, sem.at[i])
        for i, (source, target) in enumerate(zip(sources, targets))
    ]
    for copy in copies:
        copy.start()
    for copy in copies:
        copy.wait()


def shards(n, queries, keys, values, grad_out):
    rows, width = queries.shape
    shape = jax.ShapeDtypeStruct((rows, width), jnp.bfloat16)
    f32 = jnp.float32
    results = pl.pallas_call(
        functools.partial(kernel, n),
        out_shape=(pltpu.VMEM((rows, width), jnp.bfloat16),) * 4,
        in_specs=[pl.BlockSpec(memory_space=pltpu.HBM)] * 4,
        out_specs=(pl.BlockSpec(memory_space=pltpu.VMEM),) * 4,
        scratch_shapes=[
            pltpu.VMEM((4, rows, width), jnp.bfloat16),
            pltpu.VMEM((n, 2, rows, width), jnp.bfloat16),
            pltpu.VMEM((n + 1, rows, rows), f32),
            pltpu.VMEM((n + 1, rows, rows), f32),
            pltpu.VMEM((n, 8, rows), f32),
            pltpu.VMEM((rows, 128), f32),
            pltpu.VMEM((rows, 128), f32),
            pltpu.VMEM((rows, width), f32),
            pltpu.VMEM((rows, width), f32),
            pltpu.VMEM((rows, width), f32),
            pltpu.VMEM((rows, width), f32),
            pltpu.SemaphoreType.DMA((4,)),
            pltpu.SemaphoreType.DMA((n, 2)),
            pltpu.SemaphoreType.DMA((n, 2)),
            pltpu.SemaphoreType.DMA((n, 2)),
            pltpu.SemaphoreType.REGULAR,
            pltpu.SemaphoreType.DMA,
            pltpu.SemaphoreType.DMA((n,)),
            pltpu.SemaphoreType.DMA((n,)),
        ],
        compiler_params=pltpu.CompilerParams(
            collective_id=0,
            has_side_effects=True,
            vmem_limit_bytes=60 * 1024 * 1024,
        ),
    )(queries, keys, values, grad_out)
    return pl.pallas_call(
        deliver,
        out_shape=(shape,) * 4,
        in_specs=[pl.BlockSpec(memory_space=pltpu.VMEM)] * 4,
        out_specs=(pl.BlockSpec(memory_space=pltpu.HBM),) * 4,
        scratch_shapes=[pltpu.SemaphoreType.DMA((4,))],
        compiler_params=pltpu.CompilerParams(vmem_limit_bytes=2 * 1024 * 1024),
    )(*results)


def solution(mesh):
    placed = P(("grp", "ctx"), None)
    return jax.shard_map(
        functools.partial(shards, mesh.shape["ctx"]),
        mesh=mesh,
        in_specs=(placed,) * 4,
        out_specs=(placed,) * 4,
        check_vma=False,
    )
```
